1024 devices in a mesh: dp: 64 (over z, core), tensor: 16 (over x, y).
Axes of the slice: x: 4, y: 4, z: 32, core: 2. Of those that a mesh axis runs over, the one named last changes fastest.
Arguments:
- cotan: bfloat16 [8192, 4096], P(('dp', 'tensor')), may hold values from -6 to 6
- gate_pre: bfloat16 [8192, 14336], P('dp', 'tensor'), may hold values from -6 to 6
- up_pre: bfloat16 [8192, 14336], P('dp', 'tensor'), may hold values from -6 to 6
- tiles: bfloat16 [3072, 128, 128], P(('dp', 'tensor')), as said below
- tile_block: int32 [3072], P(('dp', 'tensor')), may hold values from -1 to 3583, as said below
Outputs:
- dgate: bfloat16 [8192, 14336], P('dp', 'tensor')
- dup: bfloat16 [8192, 14336], P('dp', 'tensor')
- tile_grad: float32 [3072, 128, 128], P(('dp', 'tensor'))
The draws below stay inside these ranges and needn't reach their ends.
Inputs may be any that keep to these rules, and one draw needn't show every extreme that they name: tile_block[s] is c * 32 + r for block (c, r) of w_down, or -1 for an empty slot. Every hidden block c has exactly 16 nonzero blocks, each named by exactly one slot; the slots of the device at index j of tensor name only blocks with j * 7 <= c < (j + 1) * 7, and for every index of tensor some owner has all of its 3 slots used. `tiles`: slots with tile_block -1 hold zeros.
All inputs are finite; a program needn't handle non-finite values.
Results may differ from the reference program's by a relative error of at most 0.0029.
Values may be sent and summed in bfloat16 or wider, within the bound.
No kernel may reach another device: no remote copies, remote signals or barrier semaphores. Data moves between devices by JAX's collectives and lax.ppermute only.
A program may use at most 64 MiB of HBM per device.

```python
import math
import jax
import jax.numpy as jnp
from jax import lax

D = 4096
HID = 14336
BLK = 128
TOK_DEV = 8
NBR = 32
HCT = 112
HC_DEV = 7
SLOT = 3
SLOTS = 3072
TOKENS = 8192
N_DP = 64
N_TENSOR = 16


def block_codes(key):
    half = NBR // 2
    live = HC_DEV * half
    slots_n = N_DP * SLOT
    scores = jax.random.randint(jax.random.fold_in(key, 21), (N_TENSOR, HC_DEV, NBR), 0, 1 << 20) * NBR + jnp.arange(NBR, dtype=jnp.int32)
    rows_pick = jnp.argsort(scores, axis=-1)[..., :half].astype(jnp.int32)
    column = jnp.arange(N_TENSOR * HC_DEV, dtype=jnp.int32).reshape(N_TENSOR, HC_DEV, 1)
    codes = (column * NBR + rows_pick).reshape(N_TENSOR, live)
    mixing = jax.random.randint(jax.random.fold_in(key, 22), (N_TENSOR, live), 0, 1 << 20) * live + jnp.arange(live, dtype=jnp.int32)
    codes = jnp.take_along_axis(codes, jnp.argsort(mixing, axis=-1), axis=1)
    weight = jax.random.randint(jax.random.fold_in(key, 23), (N_TENSOR, N_DP), 0, 4)
    fullest = jax.random.randint(jax.random.fold_in(key, 24), (N_TENSOR,), 0, N_DP)
    weight = jnp.where(jnp.arange(N_DP, dtype=jnp.int32)[None, :] == fullest[:, None], 8, weight)
    priority = jax.random.randint(jax.random.fold_in(key, 25), (N_TENSOR, N_DP, SLOT), 0, 1024) + weight[:, :, None] * 1024
    priority = priority.reshape(N_TENSOR, slots_n) * slots_n + jnp.arange(slots_n, dtype=jnp.int32)
    chosen = jnp.argsort(-priority, axis=-1)[:, :live]
    table = jnp.full((N_TENSOR, slots_n), -1, jnp.int32)
    table = table.at[jnp.arange(N_TENSOR, dtype=jnp.int32)[:, None], chosen].set(codes)
    return jnp.transpose(table.reshape(N_TENSOR, N_DP, SLOT), (1, 0, 2)).reshape(SLOTS).astype(jnp.int32)


def draw_tile_block(key, part):
    codes = block_codes(key)
    return codes


def draw_tiles(key, part):
    codes = block_codes(key)
    key = jax.random.fold_in(key, 5)
    scale = (D // 2) ** (-0.5)
    values = jax.random.normal(key, (SLOTS, BLK, BLK), jnp.float32)
    live_slot = (codes >= 0).astype(jnp.float32)
    return (values * (scale * live_slot)[:, None, None]).astype(jnp.bfloat16)


def block_levels(stream_key, dims, split, least, largest):
    def one(dim, blocks):
        heights = jax.random.uniform(jax.random.fold_in(jax.random.fold_in(stream_key, 6), dim), (blocks,), jnp.float32, least / len(split), largest / len(split))
        return jnp.repeat(jnp.exp(heights), dims[dim] // blocks).reshape((-1,) + (1,) * (len(dims) - dim - 1))

    factor_of = one(*split[0])
    for cut in split[1:]:
        factor_of = factor_of * one(*cut)
    return factor_of


def bell_draw(stream_key, extent, spread, reach, cuts=(), kind=jnp.bfloat16):
    entries = jax.random.normal(stream_key, extent, jnp.float32) * spread
    if len(cuts) > 0:
        entries = block_levels(stream_key, extent, cuts, -0.22, 0.18) * entries
    return jnp.clip(entries, min=-reach, max=reach).astype(kind)


def setup_inputs(seed: int = 0) -> dict:
    key_of = jax.random.split(jax.random.key(seed), 6)
    cotan = bell_draw(key_of[0], (TOKENS, D), 1.0, 6.0, ((0, 1024),))
    gate_pre = bell_draw(key_of[1], (TOKENS, HID), 1.0, 6.0, ((0, 64), (1, 16)))
    up_pre = bell_draw(key_of[2], (TOKENS, HID), 1.0, 6.0, ((0, 64), (1, 16)))
    tiles = draw_tiles(jax.random.fold_in(key_of[5], 71), 0)
    tile_block = draw_tile_block(jax.random.fold_in(key_of[5], 71), 0)
    return {"cotan": cotan, "gate_pre": gate_pre, "up_pre": up_pre, "tiles": tiles, "tile_block": tile_block}


def locate(codes, count):
    slots_n = codes.shape[0]
    match = jnp.arange(count, dtype=jnp.int32)[:, None] == codes[None, :]
    present = jnp.any(match, axis=1)
    where_at = lax.optimization_barrier(jnp.sum(jnp.where(match, jnp.arange(slots_n, dtype=jnp.int32)[None, :], 0), axis=1)).astype(jnp.int32)
    return (present, where_at)

def reference(cotan, gate_pre, up_pre, tiles, tile_block):
    count = HCT * NBR
    present, where_at = locate(tile_block, count)
    blocks = jnp.where(present[:, None, None], jnp.take(tiles, where_at, axis=0), jnp.zeros((), jnp.bfloat16))
    w_down = jnp.transpose(blocks.reshape(HCT, NBR, BLK, BLK), (0, 2, 1, 3)).reshape(HID, D)
    rows_blk = TOK_DEV * N_TENSOR
    cot_b = cotan.reshape(N_DP, rows_blk, D)
    gate_b = gate_pre.reshape(N_DP, rows_blk, HID)
    up_b = up_pre.reshape(N_DP, rows_blk, HID)

    def one_block(acc, triple):
        grads_out, gate_in, up_in = triple
        dhid = jnp.dot(grads_out, w_down.T, preferred_element_type=jnp.float32)
        gate = gate_in.astype(jnp.float32)
        upper = up_in.astype(jnp.float32)
        sigma = jax.nn.sigmoid(gate)
        silu_g = gate * sigma
        hidden = (silu_g * upper).astype(jnp.bfloat16)
        dgate = (dhid * upper * sigma * (1.0 + gate * (1.0 - sigma))).astype(jnp.bfloat16)
        dup = (dhid * silu_g).astype(jnp.bfloat16)
        acc = acc + jnp.dot(hidden.T, grads_out, preferred_element_type=jnp.float32)
        return (acc, (dgate, dup))
    acc, (dgate, dup) = lax.scan(one_block, jnp.zeros((HID, D), jnp.float32), (cot_b, gate_b, up_b))
    factor = 1.0 / math.sqrt(TOKENS)
    grad_blocks = jnp.transpose(acc.reshape(HCT, BLK, NBR, BLK), (0, 2, 1, 3)).reshape(count, BLK, BLK) * factor
    index = jnp.clip(tile_block, 0, count - 1).astype(jnp.int32)
    valid = (tile_block >= 0).astype(jnp.float32)
    tile_grad = jnp.take(grad_blocks, index, axis=0) * valid[:, None, None]
    return (dgate.reshape(TOKENS, HID), dup.reshape(TOKENS, HID), tile_grad)
```

```python
import functools
import math

import jax
import jax.numpy as jnp
from jax import lax
from jax.experimental import pallas as pl
from jax.experimental.pallas import tpu as pltpu
from jax.sharding import PartitionSpec as P

CORES = 2


def grad_kernel(owners, slots, rows_b, factor, place, codes, hid_a, hid_b, cot_a, cot_b,
                low1, high1, low2, high2, kept, hid, cot, dense):
    tokens = cot_a.shape[0]
    side = kept.shape[1]
    half = side // 2
    hid[:, :tokens] = hid_a[...]
    hid[:, tokens:] = hid_b[...]
    cot[:tokens, :] = cot_a[...]
    cot[tokens:, :] = cot_b[...]
    step = 4 * side if rows_b % 4 == 0 else side

    @pl.loop(0, rows_b * side // step)
    def _(n):
        cols = pl.ds(pl.multiple_of(n * step, side), step)
        dense[:, cols] = jnp.dot(hid[...], cot[:, cols], preferred_element_type=jnp.float32) * factor

    z = place[0]
    first = place[1]

    def block(shift, k, i, top, rows):
        owner = lax.rem(z + shift - 4 * k + 2 * owners, owners)
        code = codes[owner * slots + i]
        safe = jnp.maximum(code, first * rows_b)
        column = safe // rows_b - first
        row = lax.rem(safe, rows_b)
        value = dense[
            pl.ds(pl.multiple_of(column * side + top, half), rows),
            pl.ds(pl.multiple_of(row * side, side), side),
        ]
        return jnp.where(code >= 0, value, 0.0)

    @pl.loop(0, owners // 4)
    def _(k):
        for i in range(slots):
            at = k * slots + i
            low1[at] = block(-1, k, i, 0, side).astype(low1.dtype)
            high1[at] = block(1, k, i, 0, side).astype(high1.dtype)
            low2[at] = block(-2, k, i, 0, half).astype(low2.dtype)
            high2[at] = block(2, k, i, half, half).astype(high2.dtype)
            kept[at] = block(0, k, i, 0, side)


def token_kernel(owners, slots, rows_b, place, codes, codes_far, tiles, cot, gate_ref, up_ref,
                 dgate, dup, dense):
    side = tiles.shape[1]
    first = place[1]
    core = place[2]
    dense[...] = jnp.zeros_like(dense)

    def put(code, at):
        @pl.when(code >= 0)
        def _():
            column = code // rows_b - first
            row = lax.rem(code, rows_b)
            dense[
                pl.ds(pl.multiple_of(column * side, side), side),
                pl.ds(pl.multiple_of(row * side, side), side),
            ] = tiles[at]

    @pl.loop(0, owners)
    def _(z):
        for i in range(slots):
            put(codes[z * slots + i], (z * CORES + core) * slots + i)
            put(codes_far[z * slots + i], (z * CORES + 1 - core) * slots + i)

    @pl.loop(0, dense.shape[0] // side)
    def _(n):
        cols = pl.ds(pl.multiple_of(n * side, side), side)
        dhid = lax.dot_general(
            cot[...], dense[cols, :], (((1,), (1,)), ((), ())), preferred_element_type=jnp.float32
        )
        gate = gate_ref[:, cols].astype(jnp.float32)
        upper = up_ref[:, cols].astype(jnp.float32)
        sigma = jax.nn.sigmoid(gate)
        dgate[:, cols] = (dhid * upper * sigma * (1.0 + gate * (1.0 - sigma))).astype(dgate.dtype)
        dup[:, cols] = (dhid * (gate * sigma)).astype(dup.dtype)


def shift_z(value, by, owners):
    pairs = [
        (z * CORES + c, (z + by) % owners * CORES + c) for z in range(owners) for c in range(CORES)
    ]
    return lax.ppermute(value, "dp", pairs)


def swap_core(value, owners):
    pairs = [(z * CORES + c, z * CORES + 1 - c) for z in range(owners) for c in range(CORES)]
    return lax.ppermute(value, "dp", pairs)


def local(cotan, gate_pre, up_pre, tiles, tile_block):
    slots, side, _ = tiles.shape
    tok_dev, width = cotan.shape
    rows_b = width // side
    hid_dev = gate_pre.shape[1]
    cols_b = hid_dev // side
    owners = lax.axis_size("dp") // CORES
    members = lax.axis_size("tensor")
    tokens_n = tok_dev * members
    f32, bf16 = jnp.float32, jnp.bfloat16
    me = lax.axis_index("dp")
    core = me % CORES
    first = lax.axis_index("tensor") * cols_b
    place = jnp.stack([me // CORES, first, core]).astype(jnp.int32)

    gathered = lax.all_gather(tiles, "dp", axis=0, tiled=True)

    own = jnp.zeros((1, 1, 128), jnp.int32).at[0, 0, :slots].set(tile_block)
    rings = [[z * CORES + c for z in range(owners)] for c in range(CORES)]
    table = lax.all_to_all(
        jnp.broadcast_to(own, (owners, 1, 128)), "dp", 0, 0, tiled=True, axis_index_groups=rings
    )
    table_far = swap_core(table, owners)
    codes = table[:, 0, :slots].reshape(owners * slots)
    codes_far = table_far[:, 0, :slots].reshape(owners * slots)

    group = lax.all_to_all(
        jnp.broadcast_to(cotan[None], (members, tok_dev, width)), "tensor", 0, 0, tiled=True
    ).reshape(tokens_n, width)
    group_far = swap_core(group, owners)

    gate = gate_pre.astype(f32)
    hidden = (gate * jax.nn.sigmoid(gate) * up_pre.astype(f32)).astype(bf16).T
    hidden_far = swap_core(hidden, owners)

    factor = 1.0 / math.sqrt(tokens_n * owners * CORES)
    quarter = owners // 4 * slots
    whole = jax.ShapeDtypeStruct((quarter, side, side), bf16)
    halved = jax.ShapeDtypeStruct((quarter, side // 2, side), bf16)
    smem = pl.BlockSpec(memory_space=pltpu.SMEM)
    vmem = pl.BlockSpec(memory_space=pltpu.VMEM)
    low1, high1, low2, high2, kept = pl.pallas_call(
        functools.partial(grad_kernel, owners, slots, rows_b, factor),
        out_shape=(whole, whole, halved, halved, jax.ShapeDtypeStruct((quarter, side, side), f32)),
        in_specs=[smem, smem, vmem, vmem, vmem, vmem],
        out_specs=(vmem,) * 5,
        scratch_shapes=[
            pltpu.VMEM((hid_dev, 2 * tokens_n), bf16),
            pltpu.VMEM((2 * tokens_n, width), bf16),
            pltpu.VMEM((hid_dev, width), f32),
        ],
        compiler_params=pltpu.CompilerParams(vmem_limit_bytes=44 * 1024 * 1024),
        cost_estimate=pl.CostEstimate(
            flops=4 * hid_dev * width * tokens_n, bytes_accessed=8 * 2**20, transcendentals=0
        ),
        name="grad_blocks",
    )(place, codes, hidden, hidden_far, group, group_far)

    from_high1 = shift_z(low1, -1, owners).astype(f32)
    from_low1 = shift_z(high1, 1, owners).astype(f32)
    from_high2 = shift_z(low2, -2, owners).astype(f32)
    from_low2 = shift_z(high2, 2, owners).astype(f32)
    part = kept + from_high1 + from_low1 + jnp.concatenate([from_high2, from_low2], axis=1)
    part = part.reshape(owners // 4, slots, side, side)

    half = side // 2
    down = jnp.concatenate([part[1], part[6], part[4, :, :half]], axis=1).astype(bf16)
    up = jnp.concatenate([part[7], part[2], part[4, :, half:]], axis=1).astype(bf16)
    down_got = shift_z(down, -4, owners).astype(f32)
    up_got = shift_z(up, 4, owners).astype(f32)
    mine = part[0] + down_got[:, :side] + up_got[:, :side]
    ahead = part[3] + up_got[:, side : 2 * side]
    ahead = jnp.concatenate([ahead[:, :half] + down_got[:, 2 * side :], ahead[:, half:]], axis=1)
    behind = part[5] + down_got[:, side : 2 * side]
    behind = jnp.concatenate([behind[:, :half], behind[:, half:] + up_got[:, 2 * side :]], axis=1)
    ahead, behind = ahead.astype(bf16), behind.astype(bf16)
    gathered, codes_far, _, _ = lax.optimization_barrier((gathered, codes_far, ahead, behind))
    ahead_got = shift_z(ahead, -12, owners).astype(f32)
    behind_got = shift_z(behind, 12, owners).astype(f32)

    dgate, dup = pl.pallas_call(
        functools.partial(token_kernel, owners, slots, rows_b),
        out_shape=(jax.ShapeDtypeStruct(gate_pre.shape, bf16),) * 2,
        in_specs=[smem, smem, smem, vmem, vmem, vmem, vmem],
        out_specs=(vmem,) * 2,
        scratch_shapes=[pltpu.VMEM((hid_dev, width), bf16)],
        compiler_params=pltpu.CompilerParams(vmem_limit_bytes=40 * 1024 * 1024),
        cost_estimate=pl.CostEstimate(
            flops=2 * hid_dev * width * tokens_n, bytes_accessed=16 * 2**20, transcendentals=2**17
        ),
        name="token_grads",
    )(place, codes, codes_far, gathered, group, gate_pre, up_pre)

    mine, dgate, dup = lax.optimization_barrier((mine, dgate, dup))
    tile_grad = mine + ahead_got + behind_got
    return (dgate, dup, tile_grad)


def solution(mesh):
    placed = (
        P(("dp", "tensor"), None),
        P("dp", "tensor"),
        P("dp", "tensor"),
        P(("dp", "tensor"), None, None),
        P(("dp", "tensor")),
    )
    return jax.shard_map(
        local,
        mesh=mesh,
        in_specs=placed,
        out_specs=(P("dp", "tensor"), P("dp", "tensor"), P(("dp", "tensor"), None, None)),
        check_vma=False,
    )
```

```python
import functools
import math

import jax
import jax.numpy as jnp
from jax import lax
from jax.experimental import pallas as pl
from jax.experimental.pallas import tpu as pltpu
from jax.sharding import PartitionSpec as P

CORES = 2


def grad_kernel(owners, slots, rows_b, factor, place, codes, hid_a, hid_b, cot_a, cot_b,
                low1, high1, low2, high2, kept, hid, cot, dense):
    tokens = cot_a.shape[0]
    side = kept.shape[1]
    half = side // 2
    hid[:, :tokens] = hid_a[...]
    hid[:, tokens:] = hid_b[...]
    cot[:tokens, :] = cot_a[...]
    cot[tokens:, :] = cot_b[...]
    step = 4 * side if rows_b % 4 == 0 else side

    @pl.loop(0, rows_b * side // step)
    def _(n):
        cols = pl.ds(pl.multiple_of(n * step, side), step)
        dense[:, cols] = jnp.dot(hid[...], cot[:, cols], preferred_element_type=jnp.float32) * factor

    z = place[0]
    first = place[1]

    def block(shift, k, i, top, rows):
        owner = lax.rem(z + shift - 4 * k + 2 * owners, owners)
        code = codes[owner * slots + i]
        safe = jnp.maximum(code, first * rows_b)
        column = safe // rows_b - first
        row = lax.rem(safe, rows_b)
        value = dense[
            pl.ds(pl.multiple_of(column * side + top, half), rows),
            pl.ds(pl.multiple_of(row * side, side), side),
        ]
        return jnp.where(code >= 0, value, 0.0)

    @pl.loop(0, owners // 4)
    def _(k):
        for i in range(slots):
            at = k * slots + i
            low1[at] = block(-1, k, i, 0, side).astype(low1.dtype)
            high1[at] = block(1, k, i, 0, side).astype(high1.dtype)
            low2[at] = block(-2, k, i, 0, half).astype(low2.dtype)
            high2[at] = block(2, k, i, half, half).astype(high2.dtype)
            kept[at] = block(0, k, i, 0, side)


def token_kernel(owners, slots, rows_b, place, codes, codes_far, same, other, other_far, cot, gate_ref,
                 up_ref, dgate, dup, dense):
    side = same.shape[1]
    parity = lax.rem(place[0], 2)
    first = place[1]
    core = place[2]
    eighth = owners // 4
    dense[...] = jnp.zeros_like(dense)

    def put(code, held, tiles, at):
        @pl.when((code >= 0) & held)
        def _():
            column = code // rows_b - first
            row = lax.rem(code, rows_b)
            dense[
                pl.ds(pl.multiple_of(column * side, side), side),
                pl.ds(pl.multiple_of(row * side, side), side),
            ] = tiles[at]

    @pl.loop(0, owners // 2)
    def _(n):
        here = n // eighth == core
        for table, part in ((codes, core), (codes_far, 1 - core)):
            for i in range(slots):
                at = (n * CORES + part) * slots + i
                put(table[(2 * n + parity) * slots + i], True, same, at)
                code = table[(2 * n + 1 - parity) * slots + i]
                at = (lax.rem(n, eighth) * CORES + part) * slots + i
                put(code, here, other, at)
                put(code, jnp.logical_not(here), other_far, at)

    @pl.loop(0, dense.shape[0] // side)
    def _(n):
        cols = pl.ds(pl.multiple_of(n * side, side), side)
        dhid = lax.dot_general(
            cot[...], dense[cols, :], (((1,), (1,)), ((), ())), preferred_element_type=jnp.float32
        )
        gate = gate_ref[:, cols].astype(jnp.float32)
        upper = up_ref[:, cols].astype(jnp.float32)
        sigma = jax.nn.sigmoid(gate)
        dgate[:, cols] = (dhid * upper * sigma * (1.0 + gate * (1.0 - sigma))).astype(dgate.dtype)
        dup[:, cols] = (dhid * (gate * sigma)).astype(dup.dtype)


def shift_z(value, by, owners):
    pairs = [
        (z * CORES + c, (z + by) % owners * CORES + c) for z in range(owners) for c in range(CORES)
    ]
    return lax.ppermute(value, "dp", pairs)


def swap_core(value, owners):
    pairs = [(z * CORES + c, z * CORES + 1 - c) for z in range(owners) for c in range(CORES)]
    return lax.ppermute(value, "dp", pairs)


def local(cotan, gate_pre, up_pre, tiles, tile_block):
    slots, side, _ = tiles.shape
    tok_dev, width = cotan.shape
    rows_b = width // side
    hid_dev = gate_pre.shape[1]
    cols_b = hid_dev // side
    owners = lax.axis_size("dp") // CORES
    members = lax.axis_size("tensor")
    tokens_n = tok_dev * members
    f32, bf16 = jnp.float32, jnp.bfloat16
    me = lax.axis_index("dp")
    core = me % CORES
    first = lax.axis_index("tensor") * cols_b
    place = jnp.stack([me // CORES, first, core]).astype(jnp.int32)

    pairs = [
        [(2 * n + p) * CORES + c for n in range(owners // 2) for c in range(CORES)] for p in range(2)
    ]
    same = lax.all_gather(tiles, "dp", axis=0, tiled=True, axis_index_groups=pairs)

    own = jnp.zeros((1, 1, 128), jnp.int32).at[0, 0, :slots].set(tile_block)
    rings = [[z * CORES + c for z in range(owners)] for c in range(CORES)]
    table = lax.all_to_all(
        jnp.broadcast_to(own, (owners, 1, 128)), "dp", 0, 0, tiled=True, axis_index_groups=rings
    )
    table_far = swap_core(table, owners)
    codes = table[:, 0, :slots].reshape(owners * slots)
    codes_far = table_far[:, 0, :slots].reshape(owners * slots)

    group = lax.all_to_all(
        jnp.broadcast_to(cotan[None], (members, tok_dev, width)), "tensor", 0, 0, tiled=True
    ).reshape(tokens_n, width)
    group_far = swap_core(group, owners)

    gate = gate_pre.astype(f32)
    hidden = (gate * jax.nn.sigmoid(gate) * up_pre.astype(f32)).astype(bf16).T
    hidden_far = swap_core(hidden, owners)

    factor = 1.0 / math.sqrt(tokens_n * owners * CORES)
    quarter = owners // 4 * slots
    whole = jax.ShapeDtypeStruct((quarter, side, side), bf16)
    halved = jax.ShapeDtypeStruct((quarter, side // 2, side), bf16)
    smem = pl.BlockSpec(memory_space=pltpu.SMEM)
    vmem = pl.BlockSpec(memory_space=pltpu.VMEM)
    low1, high1, low2, high2, kept = pl.pallas_call(
        functools.partial(grad_kernel, owners, slots, rows_b, factor),
        out_shape=(whole, whole, halved, halved, jax.ShapeDtypeStruct((quarter, side, side), f32)),
        in_specs=[smem, smem, vmem, vmem, vmem, vmem],
        out_specs=(vmem,) * 5,
        scratch_shapes=[
            pltpu.VMEM((hid_dev, 2 * tokens_n), bf16),
            pltpu.VMEM((2 * tokens_n, width), bf16),
            pltpu.VMEM((hid_dev, width), f32),
        ],
        compiler_params=pltpu.CompilerParams(vmem_limit_bytes=44 * 1024 * 1024),
        cost_estimate=pl.CostEstimate(
            flops=4 * hid_dev * width * tokens_n, bytes_accessed=8 * 2**20, transcendentals=0
        ),
        name="grad_blocks",
    )(place, codes, hidden, hidden_far, group, group_far)

    from_high1 = shift_z(low1, -1, owners).astype(f32)
    from_low1 = shift_z(high1, 1, owners).astype(f32)
    from_high2 = shift_z(low2, -2, owners).astype(f32)
    from_low2 = shift_z(high2, 2, owners).astype(f32)
    part = kept + from_high1 + from_low1 + jnp.concatenate([from_high2, from_low2], axis=1)
    part = part.reshape(owners // 4, slots, side, side)

    half = side // 2
    down = jnp.concatenate([part[1], part[6], part[4, :, :half]], axis=1).astype(bf16)
    up = jnp.concatenate([part[7], part[2], part[4, :, half:]], axis=1).astype(bf16)
    same, _, _ = lax.optimization_barrier((same, down, up))
    few = owners // 4 * slots
    at = core * 2 * few
    from_back = shift_z(lax.dynamic_slice_in_dim(same, at, few), 1, owners)
    from_fore = shift_z(lax.dynamic_slice_in_dim(same, at + few, few), -1, owners)
    other = jnp.concatenate([from_back, from_fore])
    down_got = shift_z(down, -4, owners).astype(f32)
    up_got = shift_z(up, 4, owners).astype(f32)
    mine = part[0] + down_got[:, :side] + up_got[:, :side]
    ahead = part[3] + up_got[:, side : 2 * side]
    ahead = jnp.concatenate([ahead[:, :half] + down_got[:, 2 * side :], ahead[:, half:]], axis=1)
    behind = part[5] + down_got[:, side : 2 * side]
    behind = jnp.concatenate([behind[:, :half], behind[:, half:] + up_got[:, 2 * side :]], axis=1)
    ahead, behind = ahead.astype(bf16), behind.astype(bf16)
    other, codes_far, _, _ = lax.optimization_barrier((other, codes_far, ahead, behind))
    other_far = swap_core(other, owners)
    ahead_got = shift_z(ahead, -12, owners).astype(f32)
    behind_got = shift_z(behind, 12, owners).astype(f32)

    dgate, dup = pl.pallas_call(
        functools.partial(token_kernel, owners, slots, rows_b),
        out_shape=(jax.ShapeDtypeStruct(gate_pre.shape, bf16),) * 2,
        in_specs=[smem] * 3 + [vmem] * 6,
        out_specs=(vmem,) * 2,
        scratch_shapes=[pltpu.VMEM((hid_dev, width), bf16)],
        compiler_params=pltpu.CompilerParams(vmem_limit_bytes=40 * 1024 * 1024),
        cost_estimate=pl.CostEstimate(
            flops=2 * hid_dev * width * tokens_n, bytes_accessed=16 * 2**20, transcendentals=2**17
        ),
        name="token_grads",
    )(place, codes, codes_far, same, other, other_far, group, gate_pre, up_pre)

    mine, dgate, dup = lax.optimization_barrier((mine, dgate, dup))
    tile_grad = mine + ahead_got + behind_got
    return (dgate, dup, tile_grad)


def solution(mesh):
    placed = (
        P(("dp", "tensor"), None),
        P("dp", "tensor"),
        P("dp", "tensor"),
        P(("dp", "tensor"), None, None),
        P(("dp", "tensor")),
    )
    return jax.shard_map(
        local,
        mesh=mesh,
        in_specs=placed,
        out_specs=(P("dp", "tensor"), P("dp", "tensor"), P(("dp", "tensor"), None, None)),
        check_vma=False,
    )
```

```python
import functools
import math

import jax
import jax.numpy as jnp
from jax import lax
from jax.experimental import pallas as pl
from jax.experimental.pallas import tpu as pltpu
from jax.sharding import PartitionSpec as P

CORES = 2


def grad_kernel(owners, slots, rows_b, factor, place, codes, hid_a, hid_b, cot_a, cot_b,
                low1, high1, low2, high2, kept, hid, cot, dense):
    tokens = cot_a.shape[0]
    side = kept.shape[1]
    half = side // 2
    hid[:, :tokens] = hid_a[...]
    hid[:, tokens:] = hid_b[...]
    cot[:tokens, :] = cot_a[...]
    cot[tokens:, :] = cot_b[...]
    step = 4 * side if rows_b % 4 == 0 else side

    @pl.loop(0, rows_b * side // step)
    def _(n):
        cols = pl.ds(pl.multiple_of(n * step, side), step)
        dense[:, cols] = jnp.dot(hid[...], cot[:, cols], preferred_element_type=jnp.float32) * factor

    z = place[0]
    first = place[1]

    def block(shift, k, i, top, rows):
        owner = lax.rem(z + shift - 4 * k + 2 * owners, owners)
        code = codes[owner * slots + i]
        safe = jnp.maximum(code, first * rows_b)
        column = safe // rows_b - first
        row = lax.rem(safe, rows_b)
        value = dense[
            pl.ds(pl.multiple_of(column * side + top, half), rows),
            pl.ds(pl.multiple_of(row * side, side), side),
        ]
        return jnp.where(code >= 0, value, 0.0)

    @pl.loop(0, owners // 4)
    def _(k):
        for i in range(slots):
            at = k * slots + i
            low1[at] = block(-1, k, i, 0, side).astype(low1.dtype)
            high1[at] = block(1, k, i, 0, side).astype(high1.dtype)
            low2[at] = block(-2, k, i, 0, half).astype(low2.dtype)
            high2[at] = block(2, k, i, half, half).astype(high2.dtype)
            kept[at] = block(0, k, i, 0, side)


def token_kernel(owners, slots, rows_b, place, codes, codes_far, tiles, cot, gate_ref, up_ref,
                 dgate, dup, dense, arrived):
    side = tiles.shape[1]
    first = place[1]
    core = place[2]
    dense[...] = jnp.zeros_like(dense)

    def put(code, at):
        @pl.when(code >= 0)
        def _():
            column = code // rows_b - first
            row = lax.rem(code, rows_b)
            target = dense.at[
                pl.ds(pl.multiple_of(column * side, side), side),
                pl.ds(pl.multiple_of(row * side, side), side),
            ]
            pltpu.make_async_copy(tiles.at[at], target, arrived).start()

    @pl.loop(0, owners)
    def _(z):
        for i in range(slots):
            put(codes[z * slots + i], (z * CORES + core) * slots + i)
            put(codes_far[z * slots + i], (z * CORES + 1 - core) * slots + i)

    present = dense.at[: dense.shape[0] // 2]
    pltpu.make_async_copy(present, present, arrived).wait()

    @pl.loop(0, dense.shape[0] // side)
    def _(n):
        cols = pl.ds(pl.multiple_of(n * side, side), side)
        dhid = lax.dot_general(
            cot[...], dense[cols, :], (((1,), (1,)), ((), ())), preferred_element_type=jnp.float32
        )
        gate = gate_ref[:, cols].astype(jnp.float32)
        upper = up_ref[:, cols].astype(jnp.float32)
        sigma = jax.nn.sigmoid(gate)
        dgate[:, cols] = (dhid * upper * sigma * (1.0 + gate * (1.0 - sigma))).astype(dgate.dtype)
        dup[:, cols] = (dhid * (gate * sigma)).astype(dup.dtype)


def shift_z(value, by, owners):
    pairs = [
        (z * CORES + c, (z + by) % owners * CORES + c) for z in range(owners) for c in range(CORES)
    ]
    return lax.ppermute(value, "dp", pairs)


def swap_core(value, owners):
    pairs = [(z * CORES + c, z * CORES + 1 - c) for z in range(owners) for c in range(CORES)]
    return lax.ppermute(value, "dp", pairs)


def local(cotan, gate_pre, up_pre, tiles, tile_block):
    slots, side, _ = tiles.shape
    tok_dev, width = cotan.shape
    rows_b = width // side
    hid_dev = gate_pre.shape[1]
    cols_b = hid_dev // side
    owners = lax.axis_size("dp") // CORES
    members = lax.axis_size("tensor")
    tokens_n = tok_dev * members
    f32, bf16 = jnp.float32, jnp.bfloat16
    me = lax.axis_index("dp")
    core = me % CORES
    first = lax.axis_index("tensor") * cols_b
    place = jnp.stack([me // CORES, first, core]).astype(jnp.int32)

    gathered = lax.all_gather(tiles, "dp", axis=0, tiled=True)

    own = jnp.zeros((1, 1, 128), jnp.int32).at[0, 0, :slots].set(tile_block)
    rings = [[z * CORES + c for z in range(owners)] for c in range(CORES)]
    table = lax.all_to_all(
        jnp.broadcast_to(own, (owners, 1, 128)), "dp", 0, 0, tiled=True, axis_index_groups=rings
    )
    table_far = swap_core(table, owners)
    codes = table[:, 0, :slots].reshape(owners * slots)
    codes_far = table_far[:, 0, :slots].reshape(owners * slots)

    group = lax.all_to_all(
        jnp.broadcast_to(cotan[None], (members, tok_dev, width)), "tensor", 0, 0, tiled=True
    ).reshape(tokens_n, width)
    group_far = swap_core(group, owners)

    gate = gate_pre.astype(f32)
    hidden = (gate * jax.nn.sigmoid(gate) * up_pre.astype(f32)).astype(bf16).T
    hidden_far = swap_core(hidden, owners)

    factor = 1.0 / math.sqrt(tokens_n * owners * CORES)
    quarter = owners // 4 * slots
    whole = jax.ShapeDtypeStruct((quarter, side, side), bf16)
    halved = jax.ShapeDtypeStruct((quarter, side // 2, side), bf16)
    smem = pl.BlockSpec(memory_space=pltpu.SMEM)
    vmem = pl.BlockSpec(memory_space=pltpu.VMEM)
    low1, high1, low2, high2, kept = pl.pallas_call(
        functools.partial(grad_kernel, owners, slots, rows_b, factor),
        out_shape=(whole, whole, halved, halved, jax.ShapeDtypeStruct((quarter, side, side), f32)),
        in_specs=[smem, smem, vmem, vmem, vmem, vmem],
        out_specs=(vmem,) * 5,
        scratch_shapes=[
            pltpu.VMEM((hid_dev, 2 * tokens_n), bf16),
            pltpu.VMEM((2 * tokens_n, width), bf16),
            pltpu.VMEM((hid_dev, width), f32),
        ],
        compiler_params=pltpu.CompilerParams(vmem_limit_bytes=44 * 1024 * 1024),
        cost_estimate=pl.CostEstimate(
            flops=4 * hid_dev * width * tokens_n, bytes_accessed=8 * 2**20, transcendentals=0
        ),
        name="grad_blocks",
    )(place, codes, hidden, hidden_far, group, group_far)

    from_high1 = shift_z(low1, -1, owners).astype(f32)
    from_low1 = shift_z(high1, 1, owners).astype(f32)
    from_high2 = shift_z(low2, -2, owners).astype(f32)
    from_low2 = shift_z(high2, 2, owners).astype(f32)
    part = kept + from_high1 + from_low1 + jnp.concatenate([from_high2, from_low2], axis=1)
    part = part.reshape(owners // 4, slots, side, side)

    half = side // 2
    down = jnp.concatenate([part[1], part[6], part[4, :, :half]], axis=1).astype(bf16)
    up = jnp.concatenate([part[7], part[2], part[4, :, half:]], axis=1).astype(bf16)
    down_got = shift_z(down, -4, owners).astype(f32)
    up_got = shift_z(up, 4, owners).astype(f32)
    mine = part[0] + down_got[:, :side] + up_got[:, :side]
    ahead = part[3] + up_got[:, side : 2 * side]
    ahead = jnp.concatenate([ahead[:, :half] + down_got[:, 2 * side :], ahead[:, half:]], axis=1)
    behind = part[5] + down_got[:, side : 2 * side]
    behind = jnp.concatenate([behind[:, :half], behind[:, half:] + up_got[:, 2 * side :]], axis=1)
    ahead, behind = ahead.astype(bf16), behind.astype(bf16)
    gathered, codes_far, _, _ = lax.optimization_barrier((gathered, codes_far, ahead, behind))
    ahead_got = shift_z(ahead, -12, owners).astype(f32)
    behind_got = shift_z(behind, 12, owners).astype(f32)

    dgate, dup = pl.pallas_call(
        functools.partial(token_kernel, owners, slots, rows_b),
        out_shape=(jax.ShapeDtypeStruct(gate_pre.shape, bf16),) * 2,
        in_specs=[smem, smem, smem, pl.BlockSpec(memory_space=pltpu.HBM), vmem, vmem, vmem],
        out_specs=(vmem,) * 2,
        scratch_shapes=[pltpu.VMEM((hid_dev, width), bf16), pltpu.SemaphoreType.DMA],
        compiler_params=pltpu.CompilerParams(vmem_limit_bytes=60 * 1024 * 1024),
        cost_estimate=pl.CostEstimate(
            flops=2 * hid_dev * width * tokens_n, bytes_accessed=16 * 2**20, transcendentals=2**17
        ),
        name="token_grads",
    )(place, codes, codes_far, gathered, group, gate_pre, up_pre)

    mine, dgate, dup = lax.optimization_barrier((mine, dgate, dup))
    tile_grad = mine + ahead_got + behind_got
    return (dgate, dup, tile_grad)


def solution(mesh):
    placed = (
        P(("dp", "tensor"), None),
        P("dp", "tensor"),
        P("dp", "tensor"),
        P(("dp", "tensor"), None, None),
        P(("dp", "tensor")),
    )
    return jax.shard_map(
        local,
        mesh=mesh,
        in_specs=placed,
        out_specs=(P("dp", "tensor"), P("dp", "tensor"), P(("dp", "tensor"), None, None)),
        check_vma=False,
    )
```

```python
import functools
import math

import jax
import jax.numpy as jnp
from jax import lax
from jax.experimental import pallas as pl
from jax.experimental.pallas import tpu as pltpu
from jax.sharding import PartitionSpec as P

CORES = 2


def grad_kernel(owners, slots, rows_b, factor, place, codes, hid_a, hid_b, cot_a, cot_b,
                low1, high1, low2, high2, kept, hid, cot, dense):
    tokens = cot_a.shape[0]
    side = kept.shape[1]
    half = side // 2
    hid[:, :tokens] = hid_a[...]
    hid[:, tokens:] = hid_b[...]
    cot[:tokens, :] = cot_a[...]
    cot[tokens:, :] = cot_b[...]
    step = 4 * side if rows_b % 4 == 0 else side

    @pl.loop(0, rows_b * side // step)
    def _(n):
        cols = pl.ds(pl.multiple_of(n * step, side), step)
        dense[:, cols] = jnp.dot(hid[...], cot[:, cols], preferred_element_type=jnp.float32) * factor

    z = place[0]
    first = place[1]

    def block(shift, k, i, top, rows):
        owner = lax.rem(z + shift - 4 * k + 2 * owners, owners)
        code = codes[owner * slots + i]
        safe = jnp.maximum(code, first * rows_b)
        column = safe // rows_b - first
        row = lax.rem(safe, rows_b)
        value = dense[
            pl.ds(pl.multiple_of(column * side + top, half), rows),
            pl.ds(pl.multiple_of(row * side, side), side),
        ]
        return jnp.where(code >= 0, value, 0.0)

    @pl.loop(0, owners // 4)
    def _(k):
        for i in range(slots):
            at = k * slots + i
            low1[at] = block(-1, k, i, 0, side).astype(low1.dtype)
            high1[at] = block(1, k, i, 0, side).astype(high1.dtype)
            low2[at] = block(-2, k, i, 0, half).astype(low2.dtype)
            high2[at] = block(2, k, i, half, half).astype(high2.dtype)
            kept[at] = block(0, k, i, 0, side)


def token_kernel(owners, slots, rows_b, place, codes, codes_far, tiles, cot, gate_ref, up_ref,
                 dgate, dup, dense, arrived):
    side = tiles.shape[1]
    first = place[1]
    core = place[2]
    columns = dense.shape[0] // side
    split = (columns + 1) // 2
    dense[...] = jnp.zeros_like(dense)

    def put(code, at):
        @pl.when(code >= 0)
        def _():
            column = code // rows_b - first
            row = lax.rem(code, rows_b)
            target = dense.at[
                pl.ds(pl.multiple_of(column * side, side), side),
                pl.ds(pl.multiple_of(row * side, side), side),
            ]
            pltpu.make_async_copy(tiles.at[at], target, arrived.at[column // split]).start()

    @pl.loop(0, owners)
    def _(z):
        for i in range(slots):
            put(codes[z * slots + i], (z * CORES + core) * slots + i)
            put(codes_far[z * slots + i], (z * CORES + 1 - core) * slots + i)

    for part, (low, high) in enumerate(((0, split), (split, columns))):
        present = dense.at[: (high - low) * side // 2]
        pltpu.make_async_copy(present, present, arrived.at[part]).wait()
        cols = slice(low * side, high * side)
        dhid = lax.dot_general(
            cot[...], dense[cols, :], (((1,), (1,)), ((), ())), preferred_element_type=jnp.float32
        )
        gate = gate_ref[:, cols].astype(jnp.float32)
        upper = up_ref[:, cols].astype(jnp.float32)
        sigma = jax.nn.sigmoid(gate)
        dgate[:, cols] = (dhid * upper * sigma * (1.0 + gate * (1.0 - sigma))).astype(dgate.dtype)
        dup[:, cols] = (dhid * (gate * sigma)).astype(dup.dtype)


def shift_z(value, by, owners):
    pairs = [
        (z * CORES + c, (z + by) % owners * CORES + c) for z in range(owners) for c in range(CORES)
    ]
    return lax.ppermute(value, "dp", pairs)


def swap_core(value, owners):
    pairs = [(z * CORES + c, z * CORES + 1 - c) for z in range(owners) for c in range(CORES)]
    return lax.ppermute(value, "dp", pairs)


def local(cotan, gate_pre, up_pre, tiles, tile_block):
    slots, side, _ = tiles.shape
    tok_dev, width = cotan.shape
    rows_b = width // side
    hid_dev = gate_pre.shape[1]
    cols_b = hid_dev // side
    owners = lax.axis_size("dp") // CORES
    members = lax.axis_size("tensor")
    tokens_n = tok_dev * members
    f32, bf16 = jnp.float32, jnp.bfloat16
    me = lax.axis_index("dp")
    core = me % CORES
    first = lax.axis_index("tensor") * cols_b
    place = jnp.stack([me // CORES, first, core]).astype(jnp.int32)

    gathered = lax.all_gather(tiles, "dp", axis=0, tiled=True)

    own = jnp.zeros((1, 1, 128), jnp.int32).at[0, 0, :slots].set(tile_block)
    rings = [[z * CORES + c for z in range(owners)] for c in range(CORES)]
    table = lax.all_to_all(
        jnp.broadcast_to(own, (owners, 1, 128)), "dp", 0, 0, tiled=True, axis_index_groups=rings
    )
    table_far = swap_core(table, owners)
    codes = table[:, 0, :slots].reshape(owners * slots)
    codes_far = table_far[:, 0, :slots].reshape(owners * slots)

    group = lax.all_to_all(
        jnp.broadcast_to(cotan[None], (members, tok_dev, width)), "tensor", 0, 0, tiled=True
    ).reshape(tokens_n, width)
    group_far = swap_core(group, owners)

    gate = gate_pre.astype(f32)
    hidden = (gate * jax.nn.sigmoid(gate) * up_pre.astype(f32)).astype(bf16).T
    hidden_far = swap_core(hidden, owners)

    factor = 1.0 / math.sqrt(tokens_n * owners * CORES)
    quarter = owners // 4 * slots
    whole = jax.ShapeDtypeStruct((quarter, side, side), bf16)
    halved = jax.ShapeDtypeStruct((quarter, side // 2, side), bf16)
    smem = pl.BlockSpec(memory_space=pltpu.SMEM)
    vmem = pl.BlockSpec(memory_space=pltpu.VMEM)
    low1, high1, low2, high2, kept = pl.pallas_call(
        functools.partial(grad_kernel, owners, slots, rows_b, factor),
        out_shape=(whole, whole, halved, halved, jax.ShapeDtypeStruct((quarter, side, side), f32)),
        in_specs=[smem, smem, vmem, vmem, vmem, vmem],
        out_specs=(vmem,) * 5,
        scratch_shapes=[
            pltpu.VMEM((hid_dev, 2 * tokens_n), bf16),
            pltpu.VMEM((2 * tokens_n, width), bf16),
            pltpu.VMEM((hid_dev, width), f32),
        ],
        compiler_params=pltpu.CompilerParams(vmem_limit_bytes=44 * 1024 * 1024),
        cost_estimate=pl.CostEstimate(
            flops=4 * hid_dev * width * tokens_n, bytes_accessed=8 * 2**20, transcendentals=0
        ),
        name="grad_blocks",
    )(place, codes, hidden, hidden_far, group, group_far)

    from_high1 = shift_z(low1, -1, owners).astype(f32)
    from_low1 = shift_z(high1, 1, owners).astype(f32)
    from_high2 = shift_z(low2, -2, owners).astype(f32)
    from_low2 = shift_z(high2, 2, owners).astype(f32)
    part = kept + from_high1 + from_low1 + jnp.concatenate([from_high2, from_low2], axis=1)
    part = part.reshape(owners // 4, slots, side, side)

    half = side // 2
    down = jnp.concatenate([part[1], part[6], part[4, :, :half]], axis=1).astype(bf16)
    up = jnp.concatenate([part[7], part[2], part[4, :, half:]], axis=1).astype(bf16)
    down_got = shift_z(down, -4, owners).astype(f32)
    up_got = shift_z(up, 4, owners).astype(f32)
    mine = part[0] + down_got[:, :side] + up_got[:, :side]
    ahead = part[3] + up_got[:, side : 2 * side]
    ahead = jnp.concatenate([ahead[:, :half] + down_got[:, 2 * side :], ahead[:, half:]], axis=1)
    behind = part[5] + down_got[:, side : 2 * side]
    behind = jnp.concatenate([behind[:, :half], behind[:, half:] + up_got[:, 2 * side :]], axis=1)
    ahead, behind = ahead.astype(bf16), behind.astype(bf16)
    gathered, codes_far, _, _ = lax.optimization_barrier((gathered, codes_far, ahead, behind))
    ahead_got = shift_z(ahead, -12, owners).astype(f32)
    behind_got = shift_z(behind, 12, owners).astype(f32)

    dgate, dup = pl.pallas_call(
        functools.partial(token_kernel, owners, slots, rows_b),
        out_shape=(jax.ShapeDtypeStruct(gate_pre.shape, bf16),) * 2,
        in_specs=[smem, smem, smem, pl.BlockSpec(memory_space=pltpu.HBM), vmem, vmem, vmem],
        out_specs=(vmem,) * 2,
        scratch_shapes=[pltpu.VMEM((hid_dev, width), bf16), pltpu.SemaphoreType.DMA((2,))],
        compiler_params=pltpu.CompilerParams(vmem_limit_bytes=60 * 1024 * 1024),
        cost_estimate=pl.CostEstimate(
            flops=2 * hid_dev * width * tokens_n, bytes_accessed=16 * 2**20, transcendentals=2**17
        ),
        name="token_grads",
    )(place, codes, codes_far, gathered, group, gate_pre, up_pre)

    mine, dgate, dup = lax.optimization_barrier((mine, dgate, dup))
    tile_grad = mine + ahead_got + behind_got
    return (dgate, dup, tile_grad)


def solution(mesh):
    placed = (
        P(("dp", "tensor"), None),
        P("dp", "tensor"),
        P("dp", "tensor"),
        P(("dp", "tensor"), None, None),
        P(("dp", "tensor")),
    )
    return jax.shard_map(
        local,
        mesh=mesh,
        in_specs=placed,
        out_specs=(P("dp", "tensor"), P("dp", "tensor"), P(("dp", "tensor"), None, None)),
        check_vma=False,
    )
```

```python
import functools
import math

import jax
import jax.numpy as jnp
from jax import lax
from jax.experimental import pallas as pl
from jax.experimental.pallas import tpu as pltpu
from jax.sharding import PartitionSpec as P

CORES = 2


def grad_kernel(owners, slots, rows_b, factor, place, codes, hid_a, hid_b, cot_a, cot_b,
                low1, high1, low2, high2, kept, hid, cot, dense):
    tokens = cot_a.shape[0]
    side = kept.shape[1]
    half = side // 2
    hid[:, :tokens] = hid_a[...]
    hid[:, tokens:] = hid_b[...]
    cot[:tokens, :] = cot_a[...]
    cot[tokens:, :] = cot_b[...]
    step = 4 * side if rows_b % 4 == 0 else side

    @pl.loop(0, rows_b * side // step)
    def _(n):
        cols = pl.ds(pl.multiple_of(n * step, side), step)
        dense[:, cols] = jnp.dot(hid[...], cot[:, cols], preferred_element_type=jnp.float32) * factor

    z = place[0]
    first = place[1]

    def block(shift, k, i, top, rows):
        owner = lax.rem(z + shift - 4 * k + 2 * owners, owners)
        code = codes[owner * slots + i]
        safe = jnp.maximum(code, first * rows_b)
        column = safe // rows_b - first
        row = lax.rem(safe, rows_b)
        value = dense[
            pl.ds(pl.multiple_of(column * side + top, half), rows),
            pl.ds(pl.multiple_of(row * side, side), side),
        ]
        return jnp.where(code >= 0, value, 0.0)

    @pl.loop(0, owners // 4)
    def _(k):
        for i in range(slots):
            at = k * slots + i
            low1[at] = block(-1, k, i, 0, side).astype(low1.dtype)
            high1[at] = block(1, k, i, 0, side).astype(high1.dtype)
            low2[at] = block(-2, k, i, 0, half).astype(low2.dtype)
            high2[at] = block(2, k, i, half, half).astype(high2.dtype)
            kept[at] = block(0, k, i, 0, side)


def token_kernel(owners, slots, rows_b, place, codes, codes_far, tiles, cot, gate_ref, up_ref,
                 dgate, dup, dense, arrived):
    side = tiles.shape[1]
    core = place[2]
    dense[...] = jnp.zeros_like(dense)

    def put(code, at):
        @pl.when(code >= 0)
        def _():
            column = lax.div(code, rows_b)
            row = code - column * rows_b
            target = dense.at[
                pl.ds(pl.multiple_of(column * side, side), side),
                pl.ds(pl.multiple_of(row * side, side), side),
            ]
            pltpu.make_async_copy(tiles.at[at], target, arrived).start()

    @pl.loop(0, owners, unroll=4)
    def _(z):
        for i in range(slots):
            put(codes[z * slots + i], (z * CORES + core) * slots + i)
            put(codes_far[z * slots + i], (z * CORES + 1 - core) * slots + i)

    present = dense.at[: dense.shape[0] // 2]
    pltpu.make_async_copy(present, present, arrived).wait()

    @pl.loop(0, dense.shape[0] // side)
    def _(n):
        cols = pl.ds(pl.multiple_of(n * side, side), side)
        dhid = lax.dot_general(
            cot[...], dense[cols, :], (((1,), (1,)), ((), ())), preferred_element_type=jnp.float32
        )
        gate = gate_ref[:, cols].astype(jnp.float32)
        upper = up_ref[:, cols].astype(jnp.float32)
        sigma = jax.nn.sigmoid(gate)
        dgate[:, cols] = (dhid * upper * sigma * (1.0 + gate * (1.0 - sigma))).astype(dgate.dtype)
        dup[:, cols] = (dhid * (gate * sigma)).astype(dup.dtype)


def shift_z(value, by, owners):
    pairs = [
        (z * CORES + c, (z + by) % owners * CORES + c) for z in range(owners) for c in range(CORES)
    ]
    return lax.ppermute(value, "dp", pairs)


def swap_core(value, owners):
    pairs = [(z * CORES + c, z * CORES + 1 - c) for z in range(owners) for c in range(CORES)]
    return lax.ppermute(value, "dp", pairs)


def local(cotan, gate_pre, up_pre, tiles, tile_block):
    slots, side, _ = tiles.shape
    tok_dev, width = cotan.shape
    rows_b = width // side
    hid_dev = gate_pre.shape[1]
    cols_b = hid_dev // side
    owners = lax.axis_size("dp") // CORES
    members = lax.axis_size("tensor")
    tokens_n = tok_dev * members
    f32, bf16 = jnp.float32, jnp.bfloat16
    me = lax.axis_index("dp")
    core = me % CORES
    first = lax.axis_index("tensor") * cols_b
    place = jnp.stack([me // CORES, first, core]).astype(jnp.int32)

    gathered = lax.all_gather(tiles, "dp", axis=0, tiled=True)

    own = jnp.zeros((1, 1, 128), jnp.int32).at[0, 0, :slots].set(tile_block)
    rings = [[z * CORES + c for z in range(owners)] for c in range(CORES)]
    table = lax.all_to_all(
        jnp.broadcast_to(own, (owners, 1, 128)), "dp", 0, 0, tiled=True, axis_index_groups=rings
    )
    table_far = swap_core(table, owners)
    codes = table[:, 0, :slots].reshape(owners * slots)
    codes_far = table_far[:, 0, :slots].reshape(owners * slots)

    group = lax.all_to_all(
        jnp.broadcast_to(cotan[None], (members, tok_dev, width)), "tensor", 0, 0, tiled=True
    ).reshape(tokens_n, width)
    group_far = swap_core(group, owners)

    gate = gate_pre.astype(f32)
    hidden = (gate * jax.nn.sigmoid(gate) * up_pre.astype(f32)).astype(bf16).T
    hidden_far = swap_core(hidden, owners)

    factor = 1.0 / math.sqrt(tokens_n * owners * CORES)
    quarter = owners // 4 * slots
    whole = jax.ShapeDtypeStruct((quarter, side, side), bf16)
    halved = jax.ShapeDtypeStruct((quarter, side // 2, side), bf16)
    smem = pl.BlockSpec(memory_space=pltpu.SMEM)
    vmem = pl.BlockSpec(memory_space=pltpu.VMEM)
    low1, high1, low2, high2, kept = pl.pallas_call(
        functools.partial(grad_kernel, owners, slots, rows_b, factor),
        out_shape=(whole, whole, halved, halved, jax.ShapeDtypeStruct((quarter, side, side), f32)),
        in_specs=[smem, smem, vmem, vmem, vmem, vmem],
        out_specs=(vmem,) * 5,
        scratch_shapes=[
            pltpu.VMEM((hid_dev, 2 * tokens_n), bf16),
            pltpu.VMEM((2 * tokens_n, width), bf16),
            pltpu.VMEM((hid_dev, width), f32),
        ],
        compiler_params=pltpu.CompilerParams(vmem_limit_bytes=44 * 1024 * 1024),
        cost_estimate=pl.CostEstimate(
            flops=4 * hid_dev * width * tokens_n, bytes_accessed=8 * 2**20, transcendentals=0
        ),
        name="grad_blocks",
    )(place, codes, hidden, hidden_far, group, group_far)

    from_high1 = shift_z(low1, -1, owners).astype(f32)
    from_low1 = shift_z(high1, 1, owners).astype(f32)
    from_high2 = shift_z(low2, -2, owners).astype(f32)
    from_low2 = shift_z(high2, 2, owners).astype(f32)
    part = kept + from_high1 + from_low1 + jnp.concatenate([from_high2, from_low2], axis=1)
    part = part.reshape(owners // 4, slots, side, side)

    half = side // 2
    down = jnp.concatenate([part[1], part[6], part[4, :, :half]], axis=1).astype(bf16)
    up = jnp.concatenate([part[7], part[2], part[4, :, half:]], axis=1).astype(bf16)
    down_got = shift_z(down, -4, owners).astype(f32)
    up_got = shift_z(up, 4, owners).astype(f32)
    mine = part[0] + down_got[:, :side] + up_got[:, :side]
    ahead = part[3] + up_got[:, side : 2 * side]
    ahead = jnp.concatenate([ahead[:, :half] + down_got[:, 2 * side :], ahead[:, half:]], axis=1)
    behind = part[5] + down_got[:, side : 2 * side]
    behind = jnp.concatenate([behind[:, :half], behind[:, half:] + up_got[:, 2 * side :]], axis=1)
    ahead, behind = ahead.astype(bf16), behind.astype(bf16)
    def inside(table):
        return jnp.where(table >= 0, table - first * rows_b, -1)

    near, far = inside(codes), inside(codes_far)
    gathered, near, far, _, _ = lax.optimization_barrier((gathered, near, far, ahead, behind))
    ahead_got = shift_z(ahead, -12, owners).astype(f32)
    behind_got = shift_z(behind, 12, owners).astype(f32)

    dgate, dup = pl.pallas_call(
        functools.partial(token_kernel, owners, slots, rows_b),
        out_shape=(jax.ShapeDtypeStruct(gate_pre.shape, bf16),) * 2,
        in_specs=[smem, smem, smem, pl.BlockSpec(memory_space=pltpu.HBM), vmem, vmem, vmem],
        out_specs=(vmem,) * 2,
        scratch_shapes=[pltpu.VMEM((hid_dev, width), bf16), pltpu.SemaphoreType.DMA],
        compiler_params=pltpu.CompilerParams(vmem_limit_bytes=60 * 1024 * 1024),
        cost_estimate=pl.CostEstimate(
            flops=2 * hid_dev * width * tokens_n, bytes_accessed=16 * 2**20, transcendentals=2**17
        ),
        name="token_grads",
    )(place, near, far, gathered, group, gate_pre, up_pre)

    mine, dgate, dup = lax.optimization_barrier((mine, dgate, dup))
    tile_grad = mine + ahead_got + behind_got
    return (dgate, dup, tile_grad)


def solution(mesh):
    placed = (
        P(("dp", "tensor"), None),
        P("dp", "tensor"),
        P("dp", "tensor"),
        P(("dp", "tensor"), None, None),
        P(("dp", "tensor")),
    )
    return jax.shard_map(
        local,
        mesh=mesh,
        in_specs=placed,
        out_specs=(P("dp", "tensor"), P("dp", "tensor"), P(("dp", "tensor"), None, None)),
        check_vma=False,
    )
```

```python
import functools
import math

import jax
import jax.numpy as jnp
from jax import lax
from jax.experimental import pallas as pl
from jax.experimental.pallas import tpu as pltpu
from jax.sharding import PartitionSpec as P

CORES = 2


def grad_kernel(owners, slots, rows_b, factor, place, codes, hid_a, hid_b, cot_a, cot_b,
                low1, high1, low2, high2, kept, hid, cot, dense):
    tokens = cot_a.shape[0]
    side = kept.shape[1]
    half = side // 2
    hid[:, :tokens] = hid_a[...]
    hid[:, tokens:] = hid_b[...]
    cot[:tokens, :] = cot_a[...]
    cot[tokens:, :] = cot_b[...]
    step = 4 * side if rows_b % 4 == 0 else side

    @pl.loop(0, rows_b * side // step)
    def _(n):
        cols = pl.ds(pl.multiple_of(n * step, side), step)
        dense[:, cols] = jnp.dot(hid[...], cot[:, cols], preferred_element_type=jnp.float32) * factor

    z = place[0]
    first = place[1]

    def block(shift, k, i, top, rows):
        owner = lax.rem(z + shift - 4 * k + 2 * owners, owners)
        code = codes[owner * slots + i]
        safe = jnp.maximum(code, first * rows_b)
        column = safe // rows_b - first
        row = lax.rem(safe, rows_b)
        value = dense[
            pl.ds(pl.multiple_of(column * side + top, half), rows),
            pl.ds(pl.multiple_of(row * side, side), side),
        ]
        return jnp.where(code >= 0, value, 0.0)

    @pl.loop(0, owners // 4)
    def _(k):
        for i in range(slots):
            at = k * slots + i
            low1[at] = block(-1, k, i, 0, side).astype(low1.dtype)
            high1[at] = block(1, k, i, 0, side).astype(high1.dtype)
            low2[at] = block(-2, k, i, 0, half).astype(low2.dtype)
            high2[at] = block(2, k, i, half, half).astype(high2.dtype)
            kept[at] = block(0, k, i, 0, side)


def token_kernel(owners, slots, rows_b, place, codes, codes_far, tiles, cot, gate_ref, up_ref,
                 dgate, dup, dense, arrived):
    side = tiles.shape[1]
    first = place[1]
    core = place[2]
    dense[...] = jnp.zeros_like(dense)

    def put(code, at):
        @pl.when(code >= 0)
        def _():
            column = code // rows_b - first
            row = lax.rem(code, rows_b)
            target = dense.at[
                pl.ds(pl.multiple_of(column * side, side), side),
                pl.ds(pl.multiple_of(row * side, side), side),
            ]
            pltpu.make_async_copy(tiles.at[at], target, arrived).start()

    @pl.loop(0, owners)
    def _(z):
        for i in range(slots):
            put(codes[z * slots + i], (z * CORES + core) * slots + i)
            put(codes_far[z * slots + i], (z * CORES + 1 - core) * slots + i)

    present = dense.at[: dense.shape[0] // 2]
    pltpu.make_async_copy(present, present, arrived).wait()

    @pl.loop(0, dense.shape[0] // side)
    def _(n):
        cols = pl.ds(pl.multiple_of(n * side, side), side)
        dhid = lax.dot_general(
            cot[...], dense[cols, :], (((1,), (1,)), ((), ())), preferred_element_type=jnp.float32
        )
        gate = gate_ref[:, cols].astype(jnp.float32)
        upper = up_ref[:, cols].astype(jnp.float32)
        sigma = jax.nn.sigmoid(gate)
        dgate[:, cols] = (dhid * upper * sigma * (1.0 + gate * (1.0 - sigma))).astype(dgate.dtype)
        dup[:, cols] = (dhid * (gate * sigma)).astype(dup.dtype)


def shift_z(value, by, owners):
    pairs = [
        (z * CORES + c, (z + by) % owners * CORES + c) for z in range(owners) for c in range(CORES)
    ]
    return lax.ppermute(value, "dp", pairs)


def swap_core(value, owners):
    pairs = [(z * CORES + c, z * CORES + 1 - c) for z in range(owners) for c in range(CORES)]
    return lax.ppermute(value, "dp", pairs)


def local(cotan, gate_pre, up_pre, tiles, tile_block):
    slots, side, _ = tiles.shape
    tok_dev, width = cotan.shape
    rows_b = width // side
    hid_dev = gate_pre.shape[1]
    cols_b = hid_dev // side
    owners = lax.axis_size("dp") // CORES
    members = lax.axis_size("tensor")
    tokens_n = tok_dev * members
    f32, bf16 = jnp.float32, jnp.bfloat16
    me = lax.axis_index("dp")
    core = me % CORES
    first = lax.axis_index("tensor") * cols_b
    place = jnp.stack([me // CORES, first, core]).astype(jnp.int32)

    gathered = lax.all_gather(tiles, "dp", axis=0, tiled=True)

    own = jnp.zeros((1, 1, 128), jnp.int32).at[0, 0, :slots].set(tile_block)
    rings = [[z * CORES + c for z in range(owners)] for c in range(CORES)]
    table = lax.all_to_all(
        jnp.broadcast_to(own, (owners, 1, 128)), "dp", 0, 0, tiled=True, axis_index_groups=rings
    )
    table_far = swap_core(table, owners)
    codes = table[:, 0, :slots].reshape(owners * slots)
    codes_far = table_far[:, 0, :slots].reshape(owners * slots)

    group = lax.all_to_all(
        jnp.broadcast_to(cotan[None], (members, tok_dev, width)), "tensor", 0, 0, tiled=True
    ).reshape(tokens_n, width)
    group_far = swap_core(group, owners)

    gate = gate_pre.astype(f32)
    hidden = (gate * jax.nn.sigmoid(gate) * up_pre.astype(f32)).astype(bf16).T
    hidden_far = swap_core(hidden, owners)

    factor = 1.0 / math.sqrt(tokens_n * owners * CORES)
    quarter = owners // 4 * slots
    whole = jax.ShapeDtypeStruct((quarter, side, side), bf16)
    halved = jax.ShapeDtypeStruct((quarter, side // 2, side), bf16)
    smem = pl.BlockSpec(memory_space=pltpu.SMEM)
    vmem = pl.BlockSpec(memory_space=pltpu.VMEM)
    low1, high1, low2, high2, kept = pl.pallas_call(
        functools.partial(grad_kernel, owners, slots, rows_b, factor),
        out_shape=(whole, whole, halved, halved, jax.ShapeDtypeStruct((quarter, side, side), f32)),
        in_specs=[smem, smem, vmem, vmem, vmem, vmem],
        out_specs=(vmem,) * 5,
        scratch_shapes=[
            pltpu.VMEM((hid_dev, 2 * tokens_n), bf16),
            pltpu.VMEM((2 * tokens_n, width), bf16),
            pltpu.VMEM((hid_dev, width), f32),
        ],
        compiler_params=pltpu.CompilerParams(vmem_limit_bytes=44 * 1024 * 1024),
        cost_estimate=pl.CostEstimate(
            flops=4 * hid_dev * width * tokens_n, bytes_accessed=8 * 2**20, transcendentals=0
        ),
        name="grad_blocks",
    )(place, codes, hidden, hidden_far, group, group_far)

    from_high1 = shift_z(low1, -1, owners).astype(f32)
    from_low1 = shift_z(high1, 1, owners).astype(f32)
    from_high2 = shift_z(low2, -2, owners).astype(f32)
    from_low2 = shift_z(high2, 2, owners).astype(f32)
    part = kept + from_high1 + from_low1 + jnp.concatenate([from_high2, from_low2], axis=1)
    part = part.reshape(owners // 4, slots, side, side)

    half = side // 2
    down = jnp.concatenate([part[1], part[3]], axis=1).astype(bf16)
    up = jnp.concatenate([part[7], part[5]], axis=1).astype(bf16)
    far_low = shift_z(part[4, :, :half].astype(bf16), -8, owners).astype(f32)
    far_high = shift_z(part[4, :, half:].astype(bf16), 8, owners).astype(f32)
    down_got = shift_z(down, -4, owners).astype(f32)
    up_got = shift_z(up, 4, owners).astype(f32)
    mine = part[0] + down_got[:, :side] + up_got[:, :side]
    ahead = part[2] + down_got[:, side:]
    ahead = jnp.concatenate([ahead[:, :half] + far_low, ahead[:, half:]], axis=1)
    behind = part[6] + up_got[:, side:]
    behind = jnp.concatenate([behind[:, :half], behind[:, half:] + far_high], axis=1)
    ahead, behind = ahead.astype(bf16), behind.astype(bf16)
    gathered, codes_far, _, _ = lax.optimization_barrier((gathered, codes_far, ahead, behind))
    ahead_got = shift_z(ahead, -8, owners).astype(f32)
    behind_got = shift_z(behind, 8, owners).astype(f32)

    dgate, dup = pl.pallas_call(
        functools.partial(token_kernel, owners, slots, rows_b),
        out_shape=(jax.ShapeDtypeStruct(gate_pre.shape, bf16),) * 2,
        in_specs=[smem, smem, smem, pl.BlockSpec(memory_space=pltpu.HBM), vmem, vmem, vmem],
        out_specs=(vmem,) * 2,
        scratch_shapes=[pltpu.VMEM((hid_dev, width), bf16), pltpu.SemaphoreType.DMA],
        compiler_params=pltpu.CompilerParams(vmem_limit_bytes=60 * 1024 * 1024),
        cost_estimate=pl.CostEstimate(
            flops=2 * hid_dev * width * tokens_n, bytes_accessed=16 * 2**20, transcendentals=2**17
        ),
        name="token_grads",
    )(place, codes, codes_far, gathered, group, gate_pre, up_pre)

    mine, dgate, dup = lax.optimization_barrier((mine, dgate, dup))
    tile_grad = mine + ahead_got + behind_got
    return (dgate, dup, tile_grad)


def solution(mesh):
    placed = (
        P(("dp", "tensor"), None),
        P("dp", "tensor"),
        P("dp", "tensor"),
        P(("dp", "tensor"), None, None),
        P(("dp", "tensor")),
    )
    return jax.shard_map(
        local,
        mesh=mesh,
        in_specs=placed,
        out_specs=(P("dp", "tensor"), P("dp", "tensor"), P(("dp", "tensor"), None, None)),
        check_vma=False,
    )
```
